128 devices in a mesh: train: 8 (over z_hi, y), query: 16 (over z_lo, x, core).
Axes of the slice: x: 4, y: 4, z: 4 (z_hi: 2, z_lo: 2; z = z_hi * 2 + z_lo), core: 2. Of those that a mesh axis runs over, the one named last changes fastest.
Arguments:
- query_grads: bfloat16 [1024, 4096], P('query'), may hold values from -6 to 6
- precond: float32 [32, 128, 128], replicated, may hold values from -0.5 to 0.5
- train_grads: bfloat16 [262144, 4096], P(('train', 'query')), may hold values from -0.09375 to 0.09375
- query_owner: int32 [1024], replicated, may hold values from 0 to 1023, each once
Outputs:
- scores: bfloat16 [1024, 262144], P('query', 'train')
The draws below stay inside these ranges and needn't reach their ends.
Inputs may be any that keep to these rules, and one draw needn't show every extreme that they name: `query_owner`: a permutation: every output row is the row of exactly one query.
All inputs are finite; a program needn't handle non-finite values.
Results may differ from the reference program's by a relative error of at most 0.0049.
Values may be sent and summed in bfloat16 or wider, within the bound.
A program may use at most 128 MiB of HBM per device.

```python
import jax
import jax.numpy as jnp
from jax import lax

K = 4096
BLK = 128
NB = 32
QUERIES = 1024
ROWS = 262144


def shard_levels(own_key, shape, pieces, low, top_value):
    factor_of = 1.0
    for dim, blocks in pieces:
        heights = jax.random.uniform(jax.random.fold_in(jax.random.fold_in(own_key, 6), dim), (blocks,), jnp.float32, low / len(pieces), top_value / len(pieces))
        factor_of = factor_of * jnp.repeat(jnp.exp(heights), shape[dim] // blocks).reshape((-1,) + (1,) * (len(shape) - 1 - dim))
    return factor_of


def gaussian(stream_key, dims, spread, bound, cuts=(), dtype=jnp.bfloat16):
    values = spread * jax.random.normal(stream_key, dims, jnp.float32)
    if cuts:
        values = values * shard_levels(stream_key, dims, cuts, -0.22, 0.18)
    return jnp.clip(values, -bound, bound).astype(dtype)


def setup_inputs(seed: int = 0) -> dict:
    key_of = jax.random.split(jax.random.key(seed), 5)
    return {
        "query_grads": gaussian(key_of[0], (QUERIES, K), 1.0, 6.0, ((0, 16),)),
        "precond": gaussian(key_of[1], (NB, BLK, BLK), BLK ** -0.5, 0.5, (), jnp.float32),
        "train_grads": gaussian(key_of[2], (ROWS, K), K ** -0.5, 0.09375, ((0, 128),)),
        "query_owner": jax.random.permutation(key_of[3], QUERIES).astype(jnp.int32),
    }


def reference(query_grads, precond, train_grads, query_owner):
    count = query_grads.shape[0]
    split = query_grads.astype(jnp.float32).reshape(count, NB, BLK)
    conditioned = jnp.einsum("nbk,bkl->nbl", split, precond, precision=lax.Precision.HIGHEST)
    conditioned = conditioned.reshape(count, K).astype(jnp.bfloat16)
    raw = lax.dot_general(conditioned, train_grads, (((1,), (1,)), ((), ())), preferred_element_type=jnp.float32).astype(jnp.bfloat16)
    return jnp.zeros_like(raw).at[query_owner].set(raw)
```

```python
import jax
import jax.numpy as jnp
from jax import lax
from jax.experimental import pallas as pl
from jax.experimental.pallas import tpu as pltpu
from jax.sharding import PartitionSpec as P

K = 4096
BLK = 128
QUERIES = 1024
OWN = 64
LOCAL = 2048
SLICE = 512
PART = 256
GROUP = 256
GROUPS = QUERIES // GROUP
BLOCKS = GROUP // OWN
CHUNK = 512
CHUNKS = LOCAL // CHUNK
MESH = pl.DeviceIdType.MESH


def kernel(qg, pc, tr, owner, out, qv, pv, ov, cond, src, hot, gath, train, tile,
           lsem, tsem, s1s, s1r, a_s, a_r, b_s, b_r, o_s, o_r, self_sem):
    t = lax.axis_index("train")
    q = lax.axis_index("query")
    zh, y = t // 4, t % 4
    zl, x, c = q // 8, (q // 2) % 4, q % 2

    over = ((1 - zh) * 4 + y, (1 - zl) * 8 + x * 2 + c)
    up = (zh * 4 + (y + 1) % 4, q)
    down = (zh * 4 + (y + 3) % 4, q)
    mate = (t, q + 1 - 2 * c)

    def chip(dx, z):
        return z * 8 + ((x + dx) % 4) * 2

    def block_owner(g, j):
        m, b = g // 2, g % 2
        first = j // 2 == 0
        z0 = m * b
        if isinstance(j, int):
            dx = (1 - m) * (1 + 2 * b) + 2 * m if first else (1 - m) * (3 - 2 * b)
            z = z0 if first else 1 - z0
        return chip(dx, z) + j % 2

    load_q = pltpu.make_async_copy(qg.at[:, pl.ds(pl.multiple_of(t * SLICE, SLICE), SLICE)], qv, lsem.at[0])
    load_p = pltpu.make_async_copy(pc.at[pl.ds(t * 4, 4)], pv, lsem.at[1])
    load_o = pltpu.make_async_copy(owner, ov, lsem.at[2])
    load_q.start()
    load_p.start()
    load_o.start()

    def load_t(n):
        rows = pl.ds(pl.multiple_of(n * CHUNK, CHUNK), CHUNK)
        return pltpu.make_async_copy(tr.at[rows], train.at[rows], tsem.at[n])

    for n in range(CHUNKS):
        load_t(n).start()

    barrier = pltpu.get_barrier_semaphore()
    others = [(t, (q + d) % 16) for d in range(1, 16)]
    for device in others + [over, up, down]:
        pl.semaphore_signal(barrier, inc=1, device_id=device, device_id_type=MESH)

    load_q.wait()
    load_p.wait()
    for k in range(4):
        rows = qv[:, k * BLK:(k + 1) * BLK].astype(jnp.float32)
        done = jnp.dot(rows, pv[k], precision=lax.Precision.HIGHEST, preferred_element_type=jnp.float32)
        cond[k // 2, :, (k % 2) * BLK:(k % 2 + 1) * BLK] = done.astype(jnp.bfloat16)
    mine = pl.ds(pl.multiple_of(q * OWN, OWN), OWN)
    src[mine, :] = cond[c]

    pl.semaphore_wait(barrier, 18)

    def to_query(i, dest):
        return pltpu.make_async_remote_copy(
            src_ref=cond.at[dest % 2], dst_ref=src.at[mine], send_sem=s1s.at[i], recv_sem=s1r.at[q],
            device_id=(t, dest), device_id_type=MESH)

    dests = []
    for g in range(GROUPS):
        for j in range(BLOCKS):
            dests.append(block_owner(g, j))
    for i, dest in enumerate(dests):
        @pl.when(dest != q)
        def _():
            to_query(i, dest).start()

    load_o.wait()
    names = ov[...]
    for i, dest in enumerate(dests):
        row = lax.broadcasted_iota(jnp.int32, (OWN, QUERIES), 0) + dest * OWN
        hot[i * OWN:(i + 1) * OWN, :] = jnp.where(row == names, 1.0, 0.0).astype(jnp.bfloat16)

    for d in range(1, 16):
        frm = (q + d) % 16
        pltpu.make_async_remote_copy(
            src_ref=cond.at[0], dst_ref=src.at[pl.ds(pl.multiple_of(frm * OWN, OWN), OWN)],
            send_sem=s1s.at[0], recv_sem=s1r.at[frm], device_id=(t, frm), device_id_type=MESH).wait_recv()

    def piece(g, other, dy, core):
        h = zh + other * (1 - 2 * zh)
        column = (h * 4 + (y + dy) % 4) * SLICE + core * PART
        return gath.at[pl.ds(pl.multiple_of(g * GROUP, GROUP), GROUP), pl.ds(pl.multiple_of(column, PART), PART)]

    sent = ((0, 0, over), (0, 0, up), (0, 0, down), (1, 0, up), (1, 0, down), (0, 3, up), (1, 1, down))
    comes = ((1, 0), (0, 3), (0, 1), (1, 3), (1, 1), (0, 2), (1, 2))

    def link(g, i):
        other, dy, device = sent[i]
        part = piece(g, other, dy, c)
        return pltpu.make_async_remote_copy(
            src_ref=part, dst_ref=part, send_sem=a_s.at[g, i], recv_sem=a_r.at[g, i],
            device_id=device, device_id_type=MESH)

    def arrived(g, i):
        part = piece(g, *comes[i], c)
        pltpu.make_async_remote_copy(
            src_ref=part, dst_ref=part, send_sem=a_s.at[g, i], recv_sem=a_r.at[g, i],
            device_id=mate, device_id_type=MESH).wait_recv()

    pieces = ((0, 0),) + comes

    def share(g, i):
        part = piece(g, *pieces[i], c)
        return pltpu.make_async_remote_copy(
            src_ref=part, dst_ref=part, send_sem=b_s.at[g, i], recv_sem=b_r.at[g, i],
            device_id=mate, device_id_type=MESH)

    def shared(g, i):
        part = piece(g, *pieces[i], 1 - c)
        pltpu.make_async_remote_copy(
            src_ref=part, dst_ref=part, send_sem=b_s.at[g, i], recv_sem=b_r.at[g, i],
            device_id=mate, device_id_type=MESH).wait_recv()

    def order(g):
        rows = pl.ds(pl.multiple_of(g * GROUP, GROUP), GROUP)
        picked = jnp.dot(hot[rows, :], src[...], preferred_element_type=jnp.float32)
        column = pl.multiple_of(t * SLICE + c * PART, PART)
        gath[rows, pl.ds(column, PART)] = picked.astype(jnp.bfloat16)

    def step_a(g):
        link(g, 0).start()
        link(g, 1).start()
        link(g, 2).start()
        share(g, 0).start()

    def step_b(g):
        arrived(g, 0)
        link(g, 3).start()
        link(g, 4).start()
        share(g, 1).start()

    def step_c(g):
        arrived(g, 1)
        link(g, 5).start()
        share(g, 2).start()
        arrived(g, 2)
        share(g, 3).start()

    def step_d(g):
        arrived(g, 4)
        link(g, 6).start()
        share(g, 5).start()
        arrived(g, 3)
        share(g, 4).start()

    def step_e(g):
        arrived(g, 5)
        share(g, 6).start()
        arrived(g, 6)
        share(g, 7).start()
        for i in range(8):
            shared(g, i)

    order(0)
    step_a(0)
    for g in range(1, GROUPS):
        order(g)
    step_b(0)
    step_c(0)
    step_d(0)
    step_e(0)

    def deliver(g, j, n):
        dest = block_owner(g, j)
        rows = pl.ds(pl.multiple_of(g * GROUP + j * OWN, OWN), OWN)
        part = tile.at[rows, pl.ds(pl.multiple_of(n * CHUNK, CHUNK), CHUNK)]
        place = out.at[:, pl.ds(pl.multiple_of(q * LOCAL + n * CHUNK, CHUNK), CHUNK)]

        @pl.when(dest != q)
        def _():
            pltpu.make_async_remote_copy(
                src_ref=part, dst_ref=place, send_sem=o_s.at[g * BLOCKS + j], recv_sem=o_r.at[q],
                device_id=(t, dest), device_id_type=MESH).start()

        @pl.when(dest == q)
        def _():
            pltpu.make_async_copy(part, place, self_sem).start()

    def step(s, _):
        g, n = s // CHUNKS, s % CHUNKS
        after = g + 1
        more = after < GROUPS
        for k, do in enumerate((step_a, step_b, step_c, step_d)):
            @pl.when(jnp.logical_and(more, n == k))
            def _():
                do(after)

        @pl.when(g == 0)
        def _():
            load_t(n).wait()
        rows = pl.ds(pl.multiple_of(g * GROUP, GROUP), GROUP)
        cols = pl.ds(pl.multiple_of(n * CHUNK, CHUNK), CHUNK)
        scores = lax.dot_general(gath[rows, :], train[cols, :], (((1,), (1,)), ((), ())),
                                 preferred_element_type=jnp.float32)
        tile[rows, cols] = scores.astype(jnp.bfloat16)
        for j in range(BLOCKS):
            deliver(g, j, n)

        @pl.when(jnp.logical_and(more, n == CHUNKS - 1))
        def _():
            step_e(after)
        return 0

    lax.fori_loop(0, GROUPS * CHUNKS, step, 0)

    for d in range(1, 16):
        frm = (q + d) % 16
        place = out.at[:, pl.ds(pl.multiple_of(frm * LOCAL, LOCAL), LOCAL)]
        pltpu.make_async_remote_copy(
            src_ref=place, dst_ref=place, send_sem=o_s.at[0], recv_sem=o_r.at[frm],
            device_id=(t, frm), device_id_type=MESH).wait_recv()
    for i, dest in enumerate(dests):
        block = tile.at[pl.ds(i * OWN, OWN)]

        @pl.when(dest != q)
        def _():
            to_query(i, dest).wait_send()
            pltpu.make_async_remote_copy(
                src_ref=block, dst_ref=block, send_sem=o_s.at[i], recv_sem=o_r.at[q],
                device_id=(t, dest), device_id_type=MESH).wait_send()

        @pl.when(dest == q)
        def _():
            pltpu.make_async_copy(block, out.at[:, pl.ds(pl.multiple_of(q * LOCAL, LOCAL), LOCAL)], self_sem).wait()
    for g in range(GROUPS):
        for i in range(7):
            link(g, i).wait_send()
        for i in range(8):
            share(g, i).wait_send()


def per_device(query_grads, precond, train_grads, query_owner):
    dma = pltpu.SemaphoreType.DMA
    return pl.pallas_call(
        kernel,
        out_shape=jax.ShapeDtypeStruct((OWN, 16 * LOCAL), jnp.bfloat16),
        in_specs=[pl.BlockSpec(memory_space=pl.ANY)] * 4,
        out_specs=pl.BlockSpec(memory_space=pl.ANY),
        scratch_shapes=[
            pltpu.VMEM((OWN, SLICE), jnp.bfloat16),
            pltpu.VMEM((4, BLK, BLK), jnp.float32),
            pltpu.VMEM((1, QUERIES), jnp.int32),
            pltpu.VMEM((2, OWN, PART), jnp.bfloat16),
            pltpu.VMEM((QUERIES, PART), jnp.bfloat16),
            pltpu.VMEM((QUERIES, QUERIES), jnp.bfloat16),
            pltpu.VMEM((QUERIES, K), jnp.bfloat16),
            pltpu.VMEM((LOCAL, K), jnp.bfloat16),
            pltpu.VMEM((QUERIES, LOCAL), jnp.bfloat16),
            dma((3,)), dma((CHUNKS,)), dma((16,)), dma((16,)),
            dma((GROUPS, 7)), dma((GROUPS, 7)), dma((GROUPS, 8)), dma((GROUPS, 8)),
            dma((16,)), dma((16,)), dma,
        ],
        compiler_params=pltpu.CompilerParams(
            collective_id=0, has_side_effects=True, vmem_limit_bytes=56 << 20),
        cost_estimate=pl.CostEstimate(
            flops=2 * QUERIES * LOCAL * K, bytes_accessed=24 << 20, transcendentals=0),
        name="influence",
    )(query_grads, precond, train_grads, query_owner.reshape(1, QUERIES))


def solution(mesh):
    placed = (P("query", None), P(), P(("train", "query"), None), P())
    return jax.shard_map(
        per_device, mesh=mesh, in_specs=placed, out_specs=P("query", "train"), check_vma=False
    )
```

```python
import jax
import jax.numpy as jnp
from jax import lax
from jax.experimental import pallas as pl
from jax.experimental.pallas import tpu as pltpu
from jax.sharding import PartitionSpec as P

K = 4096
BLK = 128
QUERIES = 1024
OWN = 64
LOCAL = 2048
SLICE = 512
PART = 256
UNIT = 128
UNITS = QUERIES // UNIT
BLOCKS = UNIT // OWN
SINGLE = 4
CHUNK = 512
CHUNKS = LOCAL // CHUNK
MESH = pl.DeviceIdType.MESH


def kernel(qg, pc, tr, owner, out, qv, pv, ov, cond, src, hot, gath, train, tile,
           lsem, tsem, s1s, s1r, d_s, d_r, e_s, e_r, a_s, a_r, b_s, b_r, o_s, o_r, self_sem):
    t = lax.axis_index("train")
    q = lax.axis_index("query")
    zh, y = t // 4, t % 4
    zl, x, c = q // 8, (q // 2) % 4, q % 2

    over = ((1 - zh) * 4 + y, (1 - zl) * 8 + x * 2 + c)
    up = (zh * 4 + (y + 1) % 4, q)
    down = (zh * 4 + (y + 3) % 4, q)
    mate = (t, q + 1 - 2 * c)

    def apart(other, dy):
        h = zh + other * (1 - 2 * zh)
        z = zl + other * (1 - 2 * zl)
        return (h * 4 + (y + dy) % 4, z * 8 + x * 2 + c)

    ways = ((0, 1), (0, 3), (0, 2), (1, 0), (1, 1), (1, 3), (1, 2))

    def chip(dx, z):
        return z * 8 + ((x + dx) % 4) * 2

    def block_owner(u, j):
        m, b = u // 4, (u // 2) % 2
        dx = (1 - m) * (1 + 2 * b) + 2 * m if j == 0 else (1 - m) * (3 - 2 * b)
        z = m * b if j == 0 else 1 - m * b
        return chip(dx, z) + u % 2

    load_q = pltpu.make_async_copy(qg.at[:, pl.ds(pl.multiple_of(t * SLICE, SLICE), SLICE)], qv, lsem.at[0])
    load_p = pltpu.make_async_copy(pc.at[pl.ds(t * 4, 4)], pv, lsem.at[1])
    load_o = pltpu.make_async_copy(owner, ov, lsem.at[2])
    load_q.start()
    load_p.start()
    load_o.start()

    def load_t(n):
        rows = pl.ds(pl.multiple_of(n * CHUNK, CHUNK), CHUNK)
        return pltpu.make_async_copy(tr.at[rows], train.at[rows], tsem.at[n])

    barrier = pltpu.get_barrier_semaphore()
    others = [(t, (q + d) % 16) for d in range(1, 16)]
    for device in others + [apart(*way) for way in ways[:4]]:
        pl.semaphore_signal(barrier, inc=1, device_id=device, device_id_type=MESH)

    load_q.wait()
    load_p.wait()
    for k in range(4):
        rows = qv[:, k * BLK:(k + 1) * BLK].astype(jnp.float32)
        done = jnp.dot(rows, pv[k], precision=lax.Precision.HIGHEST, preferred_element_type=jnp.float32)
        cond[k % 2, k // 2] = done.astype(jnp.bfloat16)
    mine = pl.ds(pl.multiple_of(q * OWN, OWN), OWN)
    for h in range(2):
        src[h, mine, :] = cond[h, c]
    for n in range(CHUNKS):
        load_t(n).start()

    pl.semaphore_wait(barrier, 19)

    def to_query(h, dest):
        return pltpu.make_async_remote_copy(
            src_ref=cond.at[h, dest % 2], dst_ref=src.at[h, mine], send_sem=s1s.at[h], recv_sem=s1r.at[h],
            device_id=(t, dest), device_id_type=MESH)

    def queries(h):
        part = src.at[h, pl.ds(0, 15 * OWN)]
        return pltpu.make_async_remote_copy(
            src_ref=part, dst_ref=part, send_sem=s1s.at[h], recv_sem=s1r.at[h],
            device_id=mate, device_id_type=MESH)

    dests = []
    for u in range(UNITS):
        for j in range(BLOCKS):
            dests.append(block_owner(u, j))
    for h in range(2):
        for i, dest in enumerate(dests):
            @pl.when(dest != q)
            def _():
                to_query(h, dest).start()

    load_o.wait()
    names = ov[...]
    for i, dest in enumerate(dests):
        row = lax.broadcasted_iota(jnp.int32, (OWN, QUERIES), 0) + dest * OWN
        hot[i * OWN:(i + 1) * OWN, :] = jnp.where(row == names, 1.0, 0.0).astype(jnp.bfloat16)

    def unit_rows(u):
        return pl.ds(pl.multiple_of(u * UNIT, UNIT), UNIT)

    def piece(u, other, dy, core):
        h = zh + other * (1 - 2 * zh)
        column = (h * 4 + (y + dy) % 4) * SLICE + core * PART
        return gath.at[unit_rows(u), pl.ds(pl.multiple_of(column, PART), PART)]

    sent = ((0, 0, over), (0, 0, up), (0, 0, down), (1, 0, up), (1, 0, down), (0, 3, up), (1, 1, down))
    comes = ((1, 0), (0, 3), (0, 1), (1, 3), (1, 1), (0, 2), (1, 2))

    def link(u, i):
        other, dy, device = sent[i]
        part = piece(u, other, dy, c)
        return pltpu.make_async_remote_copy(
            src_ref=part, dst_ref=part, send_sem=a_s, recv_sem=a_r.at[u - 1, (0, 1, 1, 1, 1, 2, 2)[i]],
            device_id=device, device_id_type=MESH)

    def arrived(u, k):
        part = gath.at[pl.ds(0, UNIT * (1, 4, 2)[k]), pl.ds(0, PART)]
        pltpu.make_async_remote_copy(
            src_ref=part, dst_ref=part, send_sem=a_s, recv_sem=a_r.at[u - 1, k],
            device_id=mate, device_id_type=MESH).wait_recv()

    pieces = ((0, 0),) + comes

    def share(u, i):
        part = piece(u, *pieces[i], c)
        return pltpu.make_async_remote_copy(
            src_ref=part, dst_ref=part, send_sem=b_s, recv_sem=b_r.at[u - 1],
            device_id=mate, device_id_type=MESH)

    def whole(u):
        part = gath.at[pl.ds(0, 8 * UNIT), pl.ds(0, PART)]
        pltpu.make_async_remote_copy(
            src_ref=part, dst_ref=part, send_sem=b_s, recv_sem=b_r.at[u - 1],
            device_id=mate, device_id_type=MESH).wait_recv()

    def order(u, h):
        picked = jnp.dot(hot[unit_rows(u), :], src[h], preferred_element_type=jnp.float32)
        column = pl.multiple_of(t * SLICE + c * PART + h * BLK, BLK)
        gath[unit_rows(u), pl.ds(column, BLK)] = picked.astype(jnp.bfloat16)

    def half(other, dy, core, h):
        z = zh + other * (1 - 2 * zh)
        column = (z * 4 + (y + dy) % 4) * SLICE + core * PART + h * BLK
        return gath.at[pl.ds(0, UNIT), pl.ds(pl.multiple_of(column, BLK), BLK)]

    def direct(h, i):
        other, dy = ways[i]
        part = half(0, 0, c, h) if i < 4 else half(1, 0, c, h)
        return pltpu.make_async_remote_copy(
            src_ref=part, dst_ref=part, send_sem=d_s.at[h], recv_sem=d_r.at[h, i],
            device_id=apart(other, dy) if i < 4 else apart(0, dy), device_id_type=MESH)

    def came(h, i):
        part = half(ways[i][0], 4 - ways[i][1], c, h)
        pltpu.make_async_remote_copy(
            src_ref=part, dst_ref=part, send_sem=d_s.at[h], recv_sem=d_r.at[h, i],
            device_id=mate, device_id_type=MESH).wait_recv()

    def half_share(h, i):
        part = half(0, 0, c, h) if i == 7 else half(ways[i][0], 4 - ways[i][1], c, h)
        return pltpu.make_async_remote_copy(
            src_ref=part, dst_ref=part, send_sem=e_s.at[h], recv_sem=e_r.at[h],
            device_id=mate, device_id_type=MESH)

    def all_halves(h, count):
        part = src.at[h, pl.ds(0, count * UNIT)]
        return pltpu.make_async_remote_copy(
            src_ref=part, dst_ref=part, send_sem=d_s.at[h] if count == 7 else e_s.at[h], recv_sem=e_r.at[h],
            device_id=mate, device_id_type=MESH)

    def first_out(h):
        queries(h).wait_recv()
        order(0, h)
        for i in (3, 0, 1, 2):
            direct(h, i).start()
        half_share(h, 7).start()

    def first_over(h):
        came(h, 3)
        for i in (4, 5, 6):
            direct(h, i).start()
        half_share(h, 3).start()

    def first_in(h):
        for i in (0, 1, 2, 4, 5, 6):
            came(h, i)
            half_share(h, i).start()

    def own_out(u):
        link(u, 1).start()
        link(u, 2).start()
        share(u, 0).start()

    def over_out(u):
        arrived(u, 0)
        link(u, 3).start()
        link(u, 4).start()
        share(u, 1).start()

    def relay(u):
        arrived(u, 1)
        link(u, 5).start()
        link(u, 6).start()
        for i in (2, 3, 4, 5):
            share(u, i).start()

    def last(u):
        arrived(u, 2)
        share(u, 6).start()
        share(u, 7).start()

    def begin(u):
        if u + 1 < UNITS:
            link(u + 1, 0).start()
        own_out(u)
        over_out(u)

    def order_all(u):
        for h in range(2):
            order(u, h)

    first_out(0)
    first_over(0)
    first_out(1)
    for u in (1, 2):
        order_all(u)
        link(u, 0).start()
    first_over(1)
    own_out(1)
    over_out(1)
    own_out(2)
    first_in(0)
    for u in range(3, UNITS):
        order_all(u)
        if u == 3:
            link(u, 0).start()
    first_in(1)
    over_out(2)
    for h in range(2):
        all_halves(h, 8).wait_recv()

    plan = {1: (None, 1, 3), 3: (1, 2, 4), 6: (2, 3, 5), 9: (3, 4, 6), 12: (4, 5, 7),
            15: (5, 6, None), 17: (6, 7, None), 19: (7, None, None)}

    def serve(s):
        for when, (ending, passing, starting) in plan.items():
            @pl.when(s == when)
            def _():
                if ending is not None:
                    last(ending)
                if passing is not None:
                    relay(passing)
                if starting is not None:
                    begin(starting)

    def deliver(u, j, n):
        dest = block_owner(u, j)
        rows = pl.ds(pl.multiple_of(u * UNIT + j * OWN, OWN), OWN)
        part = tile.at[rows, pl.ds(pl.multiple_of(n * CHUNK, CHUNK), CHUNK)]
        place = out.at[:, pl.ds(pl.multiple_of(q * LOCAL + n * CHUNK, CHUNK), CHUNK)]

        @pl.when(dest != q)
        def _():
            pltpu.make_async_remote_copy(
                src_ref=part, dst_ref=place, send_sem=o_s, recv_sem=o_r,
                device_id=(t, dest), device_id_type=MESH).start()

        @pl.when(dest == q)
        def _():
            pltpu.make_async_copy(part, place, self_sem).start()

    def chunk_cols(n):
        return pl.ds(pl.multiple_of(n * CHUNK, CHUNK), CHUNK)

    def single(s, _):
        u, n = s // CHUNKS, s % CHUNKS

        serve(s)

        @pl.when(u == 0)
        def _():
            load_t(n).wait()
        scores = lax.dot_general(train[chunk_cols(n), :], gath[unit_rows(u), :], (((1,), (1,)), ((), ())),
                                 preferred_element_type=jnp.float32)
        tile[unit_rows(u), chunk_cols(n)] = scores.T.astype(jnp.bfloat16)
        for j in range(BLOCKS):
            deliver(u, j, n)

        @pl.when(n == CHUNKS - 1)
        def _():
            whole(u + 1)
        return 0

    lax.fori_loop(0, SINGLE * CHUNKS, single, 0)
    whole(SINGLE + 1)

    def pair(s, _):
        m, n = s // CHUNKS, s % CHUNKS
        u = SINGLE + 2 * m

        serve(s + SINGLE * CHUNKS)
        rows = pl.ds(pl.multiple_of(u * UNIT, UNIT), 2 * UNIT)
        scores = lax.dot_general(gath[rows, :], train[chunk_cols(n), :], (((1,), (1,)), ((), ())),
                                 preferred_element_type=jnp.float32)
        tile[rows, chunk_cols(n)] = scores.astype(jnp.bfloat16)
        for k in range(2):
            for j in range(BLOCKS):
                deliver(u + k, j, n)

        @pl.when(s == CHUNKS - 1)
        def _():
            whole(SINGLE + 2)
            whole(SINGLE + 3)
        return 0

    lax.fori_loop(0, 2 * CHUNKS, pair, 0)

    def ended(part, sem):
        return pltpu.make_async_remote_copy(
            src_ref=part, dst_ref=part, send_sem=sem, recv_sem=o_r, device_id=mate, device_id_type=MESH)

    for h in range(2):
        queries(h).wait_send()
        all_halves(h, 7).wait_send()
        all_halves(h, 8).wait_send()
    ended(gath.at[pl.ds(0, 7 * 7 * 16), pl.ds(0, 8 * PART)], a_s).wait_send()
    ended(gath.at[pl.ds(0, 7 * UNIT), pl.ds(0, 8 * PART)], b_s).wait_send()
    here = out.at[:, pl.ds(pl.multiple_of(q * LOCAL, LOCAL), LOCAL)]
    pltpu.make_async_copy(tile.at[pl.ds(0, OWN)], here, self_sem).wait()
    blocks = ended(tile.at[pl.ds(0, 15 * OWN)], o_s)
    blocks.wait_recv()
    blocks.wait_send()


def per_device(query_grads, precond, train_grads, query_owner):
    dma = pltpu.SemaphoreType.DMA
    return pl.pallas_call(
        kernel,
        out_shape=pltpu.VMEM((OWN, 16 * LOCAL), jnp.bfloat16),
        in_specs=[pl.BlockSpec(memory_space=pl.ANY)] * 4,
        out_specs=pl.BlockSpec(memory_space=pl.ANY),
        scratch_shapes=[
            pltpu.VMEM((OWN, SLICE), jnp.bfloat16),
            pltpu.VMEM((4, BLK, BLK), jnp.float32),
            pltpu.VMEM((1, QUERIES), jnp.int32),
            pltpu.VMEM((2, 2, OWN, BLK), jnp.bfloat16),
            pltpu.VMEM((2, QUERIES, BLK), jnp.bfloat16),
            pltpu.VMEM((QUERIES, QUERIES), jnp.bfloat16),
            pltpu.VMEM((QUERIES, K), jnp.bfloat16),
            pltpu.VMEM((LOCAL, K), jnp.bfloat16),
            pltpu.VMEM((QUERIES, LOCAL), jnp.bfloat16),
            dma((3,)), dma((CHUNKS,)), dma((2,)), dma((2,)),
            dma((2,)), dma((2, 7)), dma((2,)), dma((2,)),
            dma, dma((UNITS - 1, 3)), dma, dma((UNITS - 1,)),
            dma, dma, dma,
        ],
        compiler_params=pltpu.CompilerParams(
            collective_id=0, has_side_effects=True, vmem_limit_bytes=56 << 20),
        cost_estimate=pl.CostEstimate(
            flops=2 * QUERIES * LOCAL * K, bytes_accessed=24 << 20, transcendentals=0),
        name="influence",
    )(query_grads, precond, train_grads, query_owner.reshape(1, QUERIES))


def solution(mesh):
    placed = (P("query", None), P(), P(("train", "query"), None), P())
    return jax.shard_map(
        per_device, mesh=mesh, in_specs=placed, out_specs=P("query", "train"), check_vma=False
    )
```

```python
import jax
import jax.numpy as jnp
from jax import lax
from jax.experimental import pallas as pl
from jax.experimental.pallas import tpu as pltpu
from jax.sharding import PartitionSpec as P

K = 4096
BLK = 128
QUERIES = 1024
OWN = 64
LOCAL = 2048
SLICE = 512
PART = 256
UNIT = 128
UNITS = QUERIES // UNIT
BLOCKS = UNIT // OWN
SINGLE = 4
CHUNK = 512
CHUNKS = LOCAL // CHUNK
MESH = pl.DeviceIdType.MESH


def kernel(qg, pc, tr, owner, out, qv, pv, ov, cond, src, hot, gath, train, tile,
           lsem, tsem, s1s, s1r, d_s, d_r, e_s, e_r, a_s, a_r, b_s, b_r, o_s, o_r, self_sem):
    t = lax.axis_index("train")
    q = lax.axis_index("query")
    zh, y = t // 4, t % 4
    zl, x, c = q // 8, (q // 2) % 4, q % 2

    over = ((1 - zh) * 4 + y, (1 - zl) * 8 + x * 2 + c)
    up = (zh * 4 + (y + 1) % 4, q)
    down = (zh * 4 + (y + 3) % 4, q)
    mate = (t, q + 1 - 2 * c)

    def apart(other, dy):
        h = zh + other * (1 - 2 * zh)
        z = zl + other * (1 - 2 * zl)
        return (h * 4 + (y + dy) % 4, z * 8 + x * 2 + c)

    ways = ((0, 1), (0, 3), (0, 2), (1, 0), (1, 1), (1, 3), (1, 2))

    def chip(dx, z):
        return z * 8 + ((x + dx) % 4) * 2

    def block_owner(u, j):
        m, b = u // 4, (u // 2) % 2
        dx = (1 - m) * (1 + 2 * b) + 2 * m if j == 0 else (1 - m) * (3 - 2 * b)
        z = m * b if j == 0 else 1 - m * b
        return chip(dx, z) + u % 2

    load_q = pltpu.make_async_copy(qg.at[:, pl.ds(pl.multiple_of(t * SLICE, SLICE), SLICE)], qv, lsem.at[0])
    load_p = pltpu.make_async_copy(pc.at[pl.ds(t * 4, 4)], pv, lsem.at[1])
    load_o = pltpu.make_async_copy(owner, ov, lsem.at[2])
    load_q.start()
    load_p.start()
    load_o.start()

    def load_t(n):
        rows = pl.ds(pl.multiple_of(n * CHUNK, CHUNK), CHUNK)
        return pltpu.make_async_copy(tr.at[rows], train.at[rows], tsem.at[n])

    barrier = pltpu.get_barrier_semaphore()
    others = [(t, (q + d) % 16) for d in range(1, 16)]
    for device in others + [apart(*way) for way in ways[:4]]:
        pl.semaphore_signal(barrier, inc=1, device_id=device, device_id_type=MESH)

    load_q.wait()
    load_p.wait()
    for k in range(4):
        rows = qv[:, k * BLK:(k + 1) * BLK].astype(jnp.float32)
        done = jnp.dot(rows, pv[k], precision=lax.Precision.HIGHEST, preferred_element_type=jnp.float32)
        cond[k % 2, k // 2] = done.astype(jnp.bfloat16)
    mine = pl.ds(pl.multiple_of(q * OWN, OWN), OWN)
    for h in range(2):
        src[h, mine, :] = cond[h, c]
    for n in range(CHUNKS):
        load_t(n).start()

    pl.semaphore_wait(barrier, 19)

    def to_query(h, dest):
        return pltpu.make_async_remote_copy(
            src_ref=cond.at[h, dest % 2], dst_ref=src.at[h, mine], send_sem=s1s.at[h], recv_sem=s1r.at[h],
            device_id=(t, dest), device_id_type=MESH)

    def queries(h):
        part = src.at[h, pl.ds(0, 15 * OWN)]
        return pltpu.make_async_remote_copy(
            src_ref=part, dst_ref=part, send_sem=s1s.at[h], recv_sem=s1r.at[h],
            device_id=mate, device_id_type=MESH)

    dests = []
    for u in range(UNITS):
        for j in range(BLOCKS):
            dests.append(block_owner(u, j))
    for h in range(2):
        for dest in dests[::-1]:
            @pl.when(dest != q)
            def _():
                to_query(h, dest).start()

    load_o.wait()
    names = ov[...]
    for i, dest in enumerate(dests):
        row = lax.broadcasted_iota(jnp.int32, (OWN, QUERIES), 0) + dest * OWN
        hot[i * OWN:(i + 1) * OWN, :] = jnp.where(row == names, 1.0, 0.0).astype(jnp.bfloat16)

    def unit_rows(u):
        return pl.ds(pl.multiple_of(u * UNIT, UNIT), UNIT)

    def piece(u, other, dy, core):
        h = zh + other * (1 - 2 * zh)
        column = (h * 4 + (y + dy) % 4) * SLICE + core * PART
        return gath.at[unit_rows(u), pl.ds(pl.multiple_of(column, PART), PART)]

    sent = ((0, 0, over), (0, 0, up), (0, 0, down), (1, 0, up), (1, 0, down), (0, 3, up), (1, 1, down))
    comes = ((1, 0), (0, 3), (0, 1), (1, 3), (1, 1), (0, 2), (1, 2))

    def link(u, i):
        other, dy, device = sent[i]
        part = piece(u, other, dy, c)
        return pltpu.make_async_remote_copy(
            src_ref=part, dst_ref=part, send_sem=a_s, recv_sem=a_r.at[u - 1, (0, 1, 1, 1, 1, 2, 2)[i]],
            device_id=device, device_id_type=MESH)

    def arrived(u, k):
        part = gath.at[pl.ds(0, UNIT * (1, 4, 2)[k]), pl.ds(0, PART)]
        pltpu.make_async_remote_copy(
            src_ref=part, dst_ref=part, send_sem=a_s, recv_sem=a_r.at[u - 1, k],
            device_id=mate, device_id_type=MESH).wait_recv()

    pieces = ((0, 0),) + comes

    def share(u, i):
        part = piece(u, *pieces[i], c)
        return pltpu.make_async_remote_copy(
            src_ref=part, dst_ref=part, send_sem=b_s, recv_sem=b_r.at[u - 1],
            device_id=mate, device_id_type=MESH)

    def whole(u):
        part = gath.at[pl.ds(0, 8 * UNIT), pl.ds(0, PART)]
        pltpu.make_async_remote_copy(
            src_ref=part, dst_ref=part, send_sem=b_s, recv_sem=b_r.at[u - 1],
            device_id=mate, device_id_type=MESH).wait_recv()

    def order(u, h):
        picked = jnp.dot(hot[unit_rows(u), :], src[h], preferred_element_type=jnp.float32)
        column = pl.multiple_of(t * SLICE + c * PART + h * BLK, BLK)
        gath[unit_rows(u), pl.ds(column, BLK)] = picked.astype(jnp.bfloat16)

    def half(other, dy, core, h):
        z = zh + other * (1 - 2 * zh)
        column = (z * 4 + (y + dy) % 4) * SLICE + core * PART + h * BLK
        return gath.at[pl.ds(0, UNIT), pl.ds(pl.multiple_of(column, BLK), BLK)]

    def direct(h, i):
        other, dy = ways[i]
        part = half(0, 0, c, h) if i < 4 else half(1, 0, c, h)
        return pltpu.make_async_remote_copy(
            src_ref=part, dst_ref=part, send_sem=d_s.at[h], recv_sem=d_r.at[h, i],
            device_id=apart(other, dy) if i < 4 else apart(0, dy), device_id_type=MESH)

    def came(h, i):
        part = half(ways[i][0], 4 - ways[i][1], c, h)
        pltpu.make_async_remote_copy(
            src_ref=part, dst_ref=part, send_sem=d_s.at[h], recv_sem=d_r.at[h, i],
            device_id=mate, device_id_type=MESH).wait_recv()

    def half_share(h, i):
        part = half(0, 0, c, h) if i == 7 else half(ways[i][0], 4 - ways[i][1], c, h)
        return pltpu.make_async_remote_copy(
            src_ref=part, dst_ref=part, send_sem=e_s.at[h], recv_sem=e_r.at[h],
            device_id=mate, device_id_type=MESH)

    def all_halves(h, count):
        part = src.at[h, pl.ds(0, count * UNIT)]
        return pltpu.make_async_remote_copy(
            src_ref=part, dst_ref=part, send_sem=d_s.at[h] if count == 7 else e_s.at[h], recv_sem=e_r.at[h],
            device_id=mate, device_id_type=MESH)

    def first_out(h):
        queries(h).wait_recv()
        order(0, h)
        for i in (3, 0, 1, 2):
            direct(h, i).start()
        half_share(h, 7).start()

    def first_over(h):
        came(h, 3)
        for i in (4, 5, 6):
            direct(h, i).start()
        half_share(h, 3).start()

    def first_in(h):
        for i in (0, 1, 2, 4, 5, 6):
            came(h, i)
            half_share(h, i).start()

    def own_out(u):
        link(u, 1).start()
        link(u, 2).start()
        share(u, 0).start()

    def over_out(u):
        arrived(u, 0)
        link(u, 3).start()
        link(u, 4).start()
        share(u, 1).start()

    def relay(u):
        arrived(u, 1)
        link(u, 5).start()
        link(u, 6).start()
        for i in (2, 3, 4, 5):
            share(u, i).start()

    def last(u):
        arrived(u, 2)
        share(u, 6).start()
        share(u, 7).start()

    def begin(u):
        if u + 1 < UNITS:
            link(u + 1, 0).start()
        own_out(u)
        over_out(u)

    def order_all(u):
        for h in range(2):
            order(u, h)

    first_out(0)
    first_over(0)
    first_out(1)
    for u in (1, 2):
        order_all(u)
        link(u, 0).start()
    first_over(1)
    own_out(1)
    over_out(1)
    own_out(2)
    first_in(0)
    for u in range(3, UNITS):
        order_all(u)
        if u == 3:
            link(u, 0).start()
    first_in(1)
    over_out(2)
    for h in range(2):
        all_halves(h, 8).wait_recv()

    plan = {1: (None, 1, 3), 3: (1, 2, 4), 6: (2, 3, 5), 9: (3, 4, 6), 12: (4, 5, 7),
            15: (5, 6, None), 17: (6, 7, None), 19: (7, None, None)}

    def serve(s):
        for when, (ending, passing, starting) in plan.items():
            @pl.when(s == when)
            def _():
                if ending is not None:
                    last(ending)
                if passing is not None:
                    relay(passing)
                if starting is not None:
                    begin(starting)

    def deliver(u, j, n):
        dest = block_owner(u, j)
        rows = pl.ds(pl.multiple_of(u * UNIT + j * OWN, OWN), OWN)
        part = tile.at[rows, pl.ds(pl.multiple_of(n * CHUNK, CHUNK), CHUNK)]
        place = out.at[:, pl.ds(pl.multiple_of(q * LOCAL + n * CHUNK, CHUNK), CHUNK)]

        @pl.when(dest != q)
        def _():
            pltpu.make_async_remote_copy(
                src_ref=part, dst_ref=place, send_sem=o_s, recv_sem=o_r,
                device_id=(t, dest), device_id_type=MESH).start()

        @pl.when(dest == q)
        def _():
            pltpu.make_async_copy(part, place, self_sem).start()

    def chunk_cols(n):
        return pl.ds(pl.multiple_of(n * CHUNK, CHUNK), CHUNK)

    def single(s, _):
        u, n = s // CHUNKS, s % CHUNKS

        serve(s)

        @pl.when(u == 0)
        def _():
            load_t(n).wait()
        scores = lax.dot_general(train[chunk_cols(n), :], gath[unit_rows(u), :], (((1,), (1,)), ((), ())),
                                 preferred_element_type=jnp.float32)
        tile[unit_rows(u), chunk_cols(n)] = scores.T.astype(jnp.bfloat16)
        for j in range(BLOCKS):
            deliver(u, j, n)

        @pl.when(n == CHUNKS - 1)
        def _():
            whole(u + 1)
        return 0

    lax.fori_loop(0, SINGLE * CHUNKS, single, 0)
    whole(SINGLE + 1)

    def pair(s, _):
        m, n = s // CHUNKS, s % CHUNKS
        u = SINGLE + 2 * m

        serve(s + SINGLE * CHUNKS)
        rows = pl.ds(pl.multiple_of(u * UNIT, UNIT), 2 * UNIT)
        scores = lax.dot_general(gath[rows, :], train[chunk_cols(n), :], (((1,), (1,)), ((), ())),
                                 preferred_element_type=jnp.float32)
        tile[rows, chunk_cols(n)] = scores.astype(jnp.bfloat16)
        for k in range(2):
            for j in range(BLOCKS):
                deliver(u + k, j, n)

        @pl.when(s == CHUNKS - 1)
        def _():
            whole(SINGLE + 2)
            whole(SINGLE + 3)
        return 0

    lax.fori_loop(0, 2 * CHUNKS, pair, 0)

    def ended(part, sem):
        return pltpu.make_async_remote_copy(
            src_ref=part, dst_ref=part, send_sem=sem, recv_sem=o_r, device_id=mate, device_id_type=MESH)

    for h in range(2):
        queries(h).wait_send()
        all_halves(h, 7).wait_send()
        all_halves(h, 8).wait_send()
    ended(gath.at[pl.ds(0, 7 * 7 * 16), pl.ds(0, 8 * PART)], a_s).wait_send()
    ended(gath.at[pl.ds(0, 7 * UNIT), pl.ds(0, 8 * PART)], b_s).wait_send()
    here = out.at[:, pl.ds(pl.multiple_of(q * LOCAL, LOCAL), LOCAL)]
    pltpu.make_async_copy(tile.at[pl.ds(0, OWN)], here, self_sem).wait()
    blocks = ended(tile.at[pl.ds(0, 15 * OWN)], o_s)
    blocks.wait_recv()
    blocks.wait_send()


def per_device(query_grads, precond, train_grads, query_owner):
    dma = pltpu.SemaphoreType.DMA
    return pl.pallas_call(
        kernel,
        out_shape=pltpu.VMEM((OWN, 16 * LOCAL), jnp.bfloat16),
        in_specs=[pl.BlockSpec(memory_space=pl.ANY)] * 4,
        out_specs=pl.BlockSpec(memory_space=pl.ANY),
        scratch_shapes=[
            pltpu.VMEM((OWN, SLICE), jnp.bfloat16),
            pltpu.VMEM((4, BLK, BLK), jnp.float32),
            pltpu.VMEM((1, QUERIES), jnp.int32),
            pltpu.VMEM((2, 2, OWN, BLK), jnp.bfloat16),
            pltpu.VMEM((2, QUERIES, BLK), jnp.bfloat16),
            pltpu.VMEM((QUERIES, QUERIES), jnp.bfloat16),
            pltpu.VMEM((QUERIES, K), jnp.bfloat16),
            pltpu.VMEM((LOCAL, K), jnp.bfloat16),
            pltpu.VMEM((QUERIES, LOCAL), jnp.bfloat16),
            dma((3,)), dma((CHUNKS,)), dma((2,)), dma((2,)),
            dma((2,)), dma((2, 7)), dma((2,)), dma((2,)),
            dma, dma((UNITS - 1, 3)), dma, dma((UNITS - 1,)),
            dma, dma, dma,
        ],
        compiler_params=pltpu.CompilerParams(
            collective_id=0, has_side_effects=True, vmem_limit_bytes=56 << 20),
        cost_estimate=pl.CostEstimate(
            flops=2 * QUERIES * LOCAL * K, bytes_accessed=24 << 20, transcendentals=0),
        name="influence",
    )(query_grads, precond, train_grads, query_owner.reshape(1, QUERIES))


def solution(mesh):
    placed = (P("query", None), P(), P(("train", "query"), None), P())
    return jax.shard_map(
        per_device, mesh=mesh, in_specs=placed, out_specs=P("query", "train"), check_vma=False
    )
```

```python
import jax
import jax.numpy as jnp
from jax import lax
from jax.experimental import pallas as pl
from jax.experimental.pallas import tpu as pltpu
from jax.sharding import PartitionSpec as P

K = 4096
BLK = 128
QUERIES = 1024
OWN = 64
LOCAL = 2048
SLICE = 512
PART = 256
UNIT = 128
UNITS = QUERIES // UNIT
BLOCKS = UNIT // OWN
SINGLE = 4
CHUNK = 512
CHUNKS = LOCAL // CHUNK
MESH = pl.DeviceIdType.MESH


def kernel(qg, pc, tr, owner, out, qv, pv, ov, cond, src, hot, gath, train, tile,
           lsem, tsem, s1s, s1r, d_s, d_r, e_s, e_r, a_s, a_r, b_s, b_r, o_s, o_r, self_sem):
    t = lax.axis_index("train")
    q = lax.axis_index("query")
    zh, y = t // 4, t % 4
    zl, x, c = q // 8, (q // 2) % 4, q % 2

    over = ((1 - zh) * 4 + y, (1 - zl) * 8 + x * 2 + c)
    up = (zh * 4 + (y + 1) % 4, q)
    down = (zh * 4 + (y + 3) % 4, q)
    mate = (t, q + 1 - 2 * c)

    def apart(other, dy):
        h = zh + other * (1 - 2 * zh)
        z = zl + other * (1 - 2 * zl)
        return (h * 4 + (y + dy) % 4, z * 8 + x * 2 + c)

    ways = ((0, 1), (0, 3), (0, 2), (1, 0), (1, 1), (1, 3), (1, 2))

    def chip(dx, z):
        return z * 8 + ((x + dx) % 4) * 2

    def block_owner(u, j):
        m, b = u // 4, (u // 2) % 2
        dx = (1 - m) * (1 + 2 * b) + 2 * m if j == 0 else (1 - m) * (3 - 2 * b)
        z = m * b if j == 0 else 1 - m * b
        return chip(dx, z) + u % 2

    load_q = pltpu.make_async_copy(qg.at[:, pl.ds(pl.multiple_of(t * SLICE, SLICE), SLICE)], qv, lsem.at[0])
    load_p = pltpu.make_async_copy(pc.at[pl.ds(t * 4, 4)], pv, lsem.at[1])
    load_o = pltpu.make_async_copy(owner, ov, lsem.at[2])
    load_q.start()
    load_p.start()
    load_o.start()

    def load_t(n):
        rows = pl.ds(pl.multiple_of(n * CHUNK, CHUNK), CHUNK)
        return pltpu.make_async_copy(tr.at[rows], train.at[rows], tsem.at[n])

    barrier = pltpu.get_barrier_semaphore()
    others = [(t, (q + d) % 16) for d in range(1, 16)]
    for device in others + [apart(*way) for way in ways[:4]]:
        pl.semaphore_signal(barrier, inc=1, device_id=device, device_id_type=MESH)

    load_q.wait()
    load_p.wait()
    for k in range(4):
        rows = qv[:, k * BLK:(k + 1) * BLK].astype(jnp.float32)
        done = jnp.dot(rows, pv[k], precision=lax.Precision.HIGHEST, preferred_element_type=jnp.float32)
        cond[k % 2, k // 2] = done.astype(jnp.bfloat16)
    mine = pl.ds(pl.multiple_of(q * OWN, OWN), OWN)
    for h in range(2):
        src[h, mine, :] = cond[h, c]
    for n in range(CHUNKS):
        load_t(n).start()

    pl.semaphore_wait(barrier, 19)

    def to_query(h, dest):
        return pltpu.make_async_remote_copy(
            src_ref=cond.at[h, dest % 2], dst_ref=src.at[h, mine], send_sem=s1s.at[h], recv_sem=s1r.at[h],
            device_id=(t, dest), device_id_type=MESH)

    def queries(h):
        part = src.at[h, pl.ds(0, 15 * OWN)]
        return pltpu.make_async_remote_copy(
            src_ref=part, dst_ref=part, send_sem=s1s.at[h], recv_sem=s1r.at[h],
            device_id=mate, device_id_type=MESH)

    dests = []
    for u in range(UNITS):
        for j in range(BLOCKS):
            dests.append(block_owner(u, j))
    for h in range(2):
        for i, dest in enumerate(dests):
            @pl.when(dest != q)
            def _():
                to_query(h, dest).start()

    load_o.wait()
    names = ov[...]
    for i, dest in enumerate(dests):
        row = lax.broadcasted_iota(jnp.int32, (OWN, QUERIES), 0) + dest * OWN
        hot[i * OWN:(i + 1) * OWN, :] = jnp.where(row == names, 1.0, 0.0).astype(jnp.bfloat16)

    def unit_rows(u):
        return pl.ds(pl.multiple_of(u * UNIT, UNIT), UNIT)

    def piece(u, other, dy, core):
        h = zh + other * (1 - 2 * zh)
        column = (h * 4 + (y + dy) % 4) * SLICE + core * PART
        return gath.at[unit_rows(u), pl.ds(pl.multiple_of(column, PART), PART)]

    sent = ((0, 0, over), (0, 0, up), (0, 0, down), (1, 0, up), (1, 0, down), (0, 3, up), (1, 1, down))
    comes = ((1, 0), (0, 3), (0, 1), (1, 3), (1, 1), (0, 2), (1, 2))

    def link(u, i):
        other, dy, device = sent[i]
        part = piece(u, other, dy, c)
        return pltpu.make_async_remote_copy(
            src_ref=part, dst_ref=part, send_sem=a_s, recv_sem=a_r.at[u - 1, (0, 1, 1, 1, 1, 2, 2)[i]],
            device_id=device, device_id_type=MESH)

    def arrived(u, k):
        part = gath.at[pl.ds(0, UNIT * (1, 4, 2)[k]), pl.ds(0, PART)]
        pltpu.make_async_remote_copy(
            src_ref=part, dst_ref=part, send_sem=a_s, recv_sem=a_r.at[u - 1, k],
            device_id=mate, device_id_type=MESH).wait_recv()

    pieces = ((0, 0),) + comes

    def share(u, i):
        part = piece(u, *pieces[i], c)
        return pltpu.make_async_remote_copy(
            src_ref=part, dst_ref=part, send_sem=b_s, recv_sem=b_r.at[u - 1],
            device_id=mate, device_id_type=MESH)

    def whole(u):
        part = gath.at[pl.ds(0, 8 * UNIT), pl.ds(0, PART)]
        pltpu.make_async_remote_copy(
            src_ref=part, dst_ref=part, send_sem=b_s, recv_sem=b_r.at[u - 1],
            device_id=mate, device_id_type=MESH).wait_recv()

    def order(u, h):
        picked = jnp.dot(hot[unit_rows(u), :], src[h], preferred_element_type=jnp.float32)
        column = pl.multiple_of(t * SLICE + c * PART + h * BLK, BLK)
        gath[unit_rows(u), pl.ds(column, BLK)] = picked.astype(jnp.bfloat16)

    def half(other, dy, core, h):
        z = zh + other * (1 - 2 * zh)
        column = (z * 4 + (y + dy) % 4) * SLICE + core * PART + h * BLK
        return gath.at[pl.ds(0, UNIT), pl.ds(pl.multiple_of(column, BLK), BLK)]

    def direct(h, i):
        other, dy = ways[i]
        part = half(0, 0, c, h) if i < 4 else half(1, 0, c, h)
        return pltpu.make_async_remote_copy(
            src_ref=part, dst_ref=part, send_sem=d_s.at[h], recv_sem=d_r.at[h, i],
            device_id=apart(other, dy) if i < 4 else apart(0, dy), device_id_type=MESH)

    def came(h, i):
        part = half(ways[i][0], 4 - ways[i][1], c, h)
        pltpu.make_async_remote_copy(
            src_ref=part, dst_ref=part, send_sem=d_s.at[h], recv_sem=d_r.at[h, i],
            device_id=mate, device_id_type=MESH).wait_recv()

    def half_share(h, i):
        part = half(0, 0, c, h) if i == 7 else half(ways[i][0], 4 - ways[i][1], c, h)
        return pltpu.make_async_remote_copy(
            src_ref=part, dst_ref=part, send_sem=e_s.at[h], recv_sem=e_r.at[h],
            device_id=mate, device_id_type=MESH)

    def all_halves(h, count):
        part = src.at[h, pl.ds(0, count * UNIT)]
        return pltpu.make_async_remote_copy(
            src_ref=part, dst_ref=part, send_sem=d_s.at[h] if count == 7 else e_s.at[h], recv_sem=e_r.at[h],
            device_id=mate, device_id_type=MESH)

    def first_out(h):
        queries(h).wait_recv()
        order(0, h)
        for i in (3, 0, 1, 2):
            direct(h, i).start()
        half_share(h, 7).start()

    def first_over(h):
        came(h, 3)
        for i in (4, 5, 6):
            direct(h, i).start()
        half_share(h, 3).start()

    def first_in(h):
        for i in (0, 1, 2, 4, 5, 6):
            came(h, i)
            half_share(h, i).start()

    def own_out(u):
        link(u, 1).start()
        link(u, 2).start()
        share(u, 0).start()

    def over_out(u):
        arrived(u, 0)
        link(u, 3).start()
        link(u, 4).start()
        share(u, 1).start()

    def relay(u):
        arrived(u, 1)
        link(u, 5).start()
        link(u, 6).start()
        for i in (2, 3, 4, 5):
            share(u, i).start()

    def last(u):
        arrived(u, 2)
        share(u, 6).start()
        share(u, 7).start()

    def begin(u):
        if u + 1 < UNITS:
            link(u + 1, 0).start()
        own_out(u)
        over_out(u)

    def order_all(u):
        for h in range(2):
            order(u, h)

    first_out(0)
    first_over(0)
    first_out(1)
    for u in (1, 2):
        order_all(u)
        link(u, 0).start()
    first_over(1)
    own_out(1)
    over_out(1)
    own_out(2)
    first_in(0)
    for u in range(3, UNITS):
        order_all(u)
        if u == 3:
            link(u, 0).start()
    first_in(1)
    over_out(2)
    for h in range(2):
        all_halves(h, 8).wait_recv()

    plan = {1: (None, 1, 3), 3: (None, 2, 4), 6: (2, 3, 5), 9: (3, 4, 6), 12: (4, 5, 7),
            15: (5, 6, None), 17: (6, 7, None), 19: (7, None, None)}

    def serve(s):
        for when, (ending, passing, starting) in plan.items():
            @pl.when(s == when)
            def _():
                if passing is not None:
                    relay(passing)
                if starting is not None:
                    begin(starting)
                if ending is not None:
                    last(ending)

    def deliver(u, j, n):
        dest = block_owner(u, j)
        rows = pl.ds(pl.multiple_of(u * UNIT + j * OWN, OWN), OWN)
        part = tile.at[rows, pl.ds(pl.multiple_of(n * CHUNK, CHUNK), CHUNK)]
        place = out.at[:, pl.ds(pl.multiple_of(q * LOCAL + n * CHUNK, CHUNK), CHUNK)]

        @pl.when(dest != q)
        def _():
            pltpu.make_async_remote_copy(
                src_ref=part, dst_ref=place, send_sem=o_s, recv_sem=o_r,
                device_id=(t, dest), device_id_type=MESH).start()

        @pl.when(dest == q)
        def _():
            pltpu.make_async_copy(part, place, self_sem).start()

    def chunk_cols(n):
        return pl.ds(pl.multiple_of(n * CHUNK, CHUNK), CHUNK)

    def single(s, _):
        u, n = s // CHUNKS, s % CHUNKS

        serve(s)

        @pl.when(u == 0)
        def _():
            load_t(n).wait()
        scores = lax.dot_general(train[chunk_cols(n), :], gath[unit_rows(u), :], (((1,), (1,)), ((), ())),
                                 preferred_element_type=jnp.float32)
        tile[unit_rows(u), chunk_cols(n)] = scores.T.astype(jnp.bfloat16)
        for j in range(BLOCKS):
            deliver(u, j, n)

        @pl.when(s == CHUNKS - 1)
        def _():
            last(1)

        @pl.when(n == CHUNKS - 1)
        def _():
            whole(u + 1)
        return 0

    lax.fori_loop(0, SINGLE * CHUNKS, single, 0)
    whole(SINGLE + 1)

    def pair(s, _):
        m, n = s // CHUNKS, s % CHUNKS
        u = SINGLE + 2 * m

        serve(s + SINGLE * CHUNKS)
        rows = pl.ds(pl.multiple_of(u * UNIT, UNIT), 2 * UNIT)
        scores = lax.dot_general(gath[rows, :], train[chunk_cols(n), :], (((1,), (1,)), ((), ())),
                                 preferred_element_type=jnp.float32)
        tile[rows, chunk_cols(n)] = scores.astype(jnp.bfloat16)
        for k in range(2):
            for j in range(BLOCKS):
                deliver(u + k, j, n)

        @pl.when(s == CHUNKS - 1)
        def _():
            whole(SINGLE + 2)
            whole(SINGLE + 3)
        return 0

    lax.fori_loop(0, 2 * CHUNKS, pair, 0)

    def ended(part, sem):
        return pltpu.make_async_remote_copy(
            src_ref=part, dst_ref=part, send_sem=sem, recv_sem=o_r, device_id=mate, device_id_type=MESH)

    for h in range(2):
        queries(h).wait_send()
        all_halves(h, 7).wait_send()
        all_halves(h, 8).wait_send()
    ended(gath.at[pl.ds(0, 7 * 7 * 16), pl.ds(0, 8 * PART)], a_s).wait_send()
    ended(gath.at[pl.ds(0, 7 * UNIT), pl.ds(0, 8 * PART)], b_s).wait_send()
    here = out.at[:, pl.ds(pl.multiple_of(q * LOCAL, LOCAL), LOCAL)]
    pltpu.make_async_copy(tile.at[pl.ds(0, OWN)], here, self_sem).wait()
    blocks = ended(tile.at[pl.ds(0, 15 * OWN)], o_s)
    blocks.wait_recv()
    blocks.wait_send()


def per_device(query_grads, precond, train_grads, query_owner):
    dma = pltpu.SemaphoreType.DMA
    return pl.pallas_call(
        kernel,
        out_shape=pltpu.VMEM((OWN, 16 * LOCAL), jnp.bfloat16),
        in_specs=[pl.BlockSpec(memory_space=pl.ANY)] * 4,
        out_specs=pl.BlockSpec(memory_space=pl.ANY),
        scratch_shapes=[
            pltpu.VMEM((OWN, SLICE), jnp.bfloat16),
            pltpu.VMEM((4, BLK, BLK), jnp.float32),
            pltpu.VMEM((1, QUERIES), jnp.int32),
            pltpu.VMEM((2, 2, OWN, BLK), jnp.bfloat16),
            pltpu.VMEM((2, QUERIES, BLK), jnp.bfloat16),
            pltpu.VMEM((QUERIES, QUERIES), jnp.bfloat16),
            pltpu.VMEM((QUERIES, K), jnp.bfloat16),
            pltpu.VMEM((LOCAL, K), jnp.bfloat16),
            pltpu.VMEM((QUERIES, LOCAL), jnp.bfloat16),
            dma((3,)), dma((CHUNKS,)), dma((2,)), dma((2,)),
            dma((2,)), dma((2, 7)), dma((2,)), dma((2,)),
            dma, dma((UNITS - 1, 3)), dma, dma((UNITS - 1,)),
            dma, dma, dma,
        ],
        compiler_params=pltpu.CompilerParams(
            collective_id=0, has_side_effects=True, vmem_limit_bytes=56 << 20),
        cost_estimate=pl.CostEstimate(
            flops=2 * QUERIES * LOCAL * K, bytes_accessed=24 << 20, transcendentals=0),
        name="influence",
    )(query_grads, precond, train_grads, query_owner.reshape(1, QUERIES))


def solution(mesh):
    placed = (P("query", None), P(), P(("train", "query"), None), P())
    return jax.shard_map(
        per_device, mesh=mesh, in_specs=placed, out_specs=P("query", "train"), check_vma=False
    )
```
